32 devices in a mesh: row: 8 (over z, y), col: 4 (over x, core).
Axes of the slice: x: 2, y: 2, z: 4, core: 2. Of those that a mesh axis runs over, the one named last changes fastest.
Arguments:
- weights: bfloat16 [24576, 24576], P('row', 'col'), may hold values from -0.0390625 to 0.0390625
- rates: bfloat16 [5, 24576, 128], P(None, 'col'), may hold values from -0.94921875 to 0.94921875
Outputs:
- weight_grad: bfloat16 [24576, 24576], P('row', 'col')
The draws below stay inside these ranges and needn't reach their ends.
All inputs are finite; a program needn't handle non-finite values.
Results may differ from the reference program's by a relative error of at most 0.02.
Values may be sent and summed in bfloat16 or wider, within the bound.
A program may use at most 384 MiB of HBM per device.

```python
import jax
import jax.numpy as jnp
from jax import lax

UNITS = 24576
TRIALS = 128
STEPS = 4


def block_scale(key, extent, shards, smallest, high):
    level, own = 1.0, jax.random.fold_in(key, 6)
    for axis_at, blocks in shards:
        draws = jnp.exp(jax.random.uniform(jax.random.fold_in(own, axis_at), (blocks,), jnp.float32, smallest / len(shards), high / len(shards)))
        level = level * jnp.repeat(draws, extent[axis_at] // blocks).reshape([-1 if axis == axis_at else 1 for axis in range(len(extent))])
    return level


def noise(stream_key, extent, spread, bound, pieces=(), held_as=jnp.bfloat16):
    loudness = block_scale(stream_key, extent, pieces, -0.22, 0.18) if pieces else 1.0
    entries = jax.random.normal(stream_key, extent, jnp.float32) * spread * loudness
    return jnp.minimum(jnp.maximum(entries, -bound), bound).astype(held_as)


def setup_inputs(seed: int = 0) -> dict:
    streams_of = jax.random.split(jax.random.key(seed), 3)
    weights = noise(streams_of[0], (UNITS, UNITS), UNITS ** -0.5, 0.0390625, ((0, 8), (1, 4)))
    rates = jnp.clip(jax.random.uniform(streams_of[1], (STEPS + 1, UNITS, TRIALS), jnp.float32, -0.94921875, 0.94921875) * block_scale(streams_of[1], (STEPS + 1, UNITS, TRIALS), ((1, 4),), -0.4, 0.0), -0.94921875, 0.94921875).astype(jnp.bfloat16)
    return dict(weights=weights, rates=rates)


def reference(weights, rates):
    ratef = rates.astype(jnp.float32)
    adjoint = ratef[STEPS] - ratef[0]
    grads = []
    for step in range(STEPS, 0, -1):
        local_grad = (adjoint * (1.0 - ratef[step] * ratef[step])).astype(jnp.bfloat16)
        grads.append(local_grad)
        if step > 1:
            adjoint = lax.dot_general(weights, local_grad, (((0,), (0,)), ((), ())), preferred_element_type=jnp.float32)
    stacked = jnp.concatenate(grads, axis=1)
    previous = jnp.concatenate([rates[step - 1] for step in range(STEPS, 0, -1)], axis=1)
    blocks = stacked.reshape(32, UNITS // 32, stacked.shape[1])

    def one_block(block):
        full = lax.dot_general(block, previous, (((1,), (1,)), ((), ())), preferred_element_type=jnp.float32)
        return full.astype(jnp.bfloat16)

    return lax.map(one_block, blocks).reshape(UNITS, UNITS)
```

```python
import jax
import jax.numpy as jnp
from jax import lax
from jax.sharding import PartitionSpec as P

STEPS = 4


def per_device(rows, cols, weights, rates):
    chunk = weights.shape[1] // rows
    row_index = lax.axis_index("row")
    exchange = [(r * cols + c, c * rows + r) for r in range(rows) for c in range(cols)]
    own = lax.dynamic_slice_in_dim(rates, row_index * chunk, chunk, 1).astype(jnp.float32)

    def local_grad(adjoint, step):
        return (adjoint * (1.0 - own[step] * own[step])).astype(jnp.bfloat16)

    def spread(piece):
        moved = lax.ppermute(piece, ("row", "col"), exchange)
        return lax.all_gather(moved, "col", axis=0, tiled=True)

    grad = spread(local_grad(own[STEPS] - own[0], STEPS))
    grads = [grad]
    for step in range(STEPS, 1, -1):
        partial_sum = lax.dot_general(
            weights, grad, (((0,), (0,)), ((), ())), preferred_element_type=jnp.float32
        ).astype(jnp.bfloat16)
        split = partial_sum.reshape(rows, chunk, -1)
        split = lax.all_to_all(split, "row", split_axis=0, concat_axis=0)
        adjoint = jnp.sum(split.astype(jnp.float32), axis=0)
        grad = spread(local_grad(adjoint.astype(jnp.float32), step - 1))
        grads.append(grad)
    stacked = jnp.concatenate(grads, axis=1)
    previous = jnp.concatenate([rates[step - 1] for step in range(STEPS, 0, -1)], axis=1)
    return lax.dot_general(
        stacked, previous, (((1,), (1,)), ((), ())), preferred_element_type=jnp.float32
    ).astype(jnp.bfloat16)


def solution(mesh):
    rows, cols = mesh.shape["row"], mesh.shape["col"]

    def body(weights, rates):
        return per_device(rows, cols, weights, rates)

    return jax.shard_map(
        body, mesh=mesh, in_specs=(P("row", "col"), P(None, "col", None)),
        out_specs=P("row", "col"), check_vma=False
    )
```

```python
import functools

import jax
import jax.numpy as jnp
from jax import lax
from jax.experimental import pallas as pl
from jax.experimental.pallas import tpu as pltpu
from jax.sharding import PartitionSpec as P

STEPS = 4


def exchange_kernel(
    rows, part_ref, own_ref, out_ref,
    halves, merged, landed, total, pair_send, pair_recv, send_sem, recv_sem,
):
    row, col = lax.axis_index("row"), lax.axis_index("col")
    mesh_ids = pl.DeviceIdType.MESH
    groups, parity, group = rows // 2, row % 2, row // 2
    pair = row + 1 - 2 * parity
    order = list(range(1, groups)) + [0]
    paired, sums = {}, {}

    barrier = pltpu.get_barrier_semaphore()
    for peer in [pair] + [2 * ((group + turn) % groups) + parity for turn in range(1, groups)]:
        pl.semaphore_signal(barrier, inc=1, device_id=(peer, col), device_id_type=mesh_ids)
    pl.semaphore_wait(barrier, groups)

    for turn in order:
        owner = 2 * ((group + turn) % groups)
        paired[turn] = pltpu.make_async_remote_copy(
            src_ref=part_ref.at[owner + 1 - parity], dst_ref=halves.at[turn],
            send_sem=pair_send.at[turn], recv_sem=pair_recv.at[turn],
            device_id=(pair, col), device_id_type=mesh_ids,
        )
        paired[turn].start()
    for turn in order:
        owner = 2 * ((group + turn) % groups) + parity
        paired[turn].wait_recv()
        both = part_ref[owner].astype(jnp.float32) + halves[turn].astype(jnp.float32)
        if turn:
            merged[turn] = both.astype(jnp.bfloat16)
            sums[turn] = pltpu.make_async_remote_copy(
                src_ref=merged.at[turn], dst_ref=landed.at[turn],
                send_sem=send_sem.at[turn], recv_sem=recv_sem.at[turn],
                device_id=(owner, col), device_id_type=mesh_ids,
            )
            sums[turn].start()
        else:
            total[...] = both
    for turn in sums:
        sums[turn].wait_recv()
        total[...] += landed[turn].astype(jnp.float32)
    own = own_ref[...].astype(jnp.float32)
    out_ref[...] = (total[...] * (1.0 - own * own)).astype(jnp.bfloat16)
    for copy in list(paired.values()) + list(sums.values()):
        copy.wait_send()


def exchange_sum(rows, parts, own):
    chunk, trials = own.shape
    vmem = pl.BlockSpec(memory_space=pltpu.VMEM)
    return pl.pallas_call(
        functools.partial(exchange_kernel, rows),
        out_shape=jax.ShapeDtypeStruct((chunk, trials), jnp.bfloat16),
        in_specs=[vmem, vmem],
        out_specs=vmem,
        scratch_shapes=[
            pltpu.VMEM((rows // 2, chunk, trials), jnp.bfloat16),
            pltpu.VMEM((rows // 2, chunk, trials), jnp.bfloat16),
            pltpu.VMEM((rows // 2, chunk, trials), jnp.bfloat16),
            pltpu.VMEM((chunk, trials), jnp.float32),
            pltpu.SemaphoreType.DMA((rows // 2,)),
            pltpu.SemaphoreType.DMA((rows // 2,)),
            pltpu.SemaphoreType.DMA((rows // 2,)),
            pltpu.SemaphoreType.DMA((rows // 2,)),
        ],
        compiler_params=pltpu.CompilerParams(
            collective_id=0, has_side_effects=True, vmem_limit_bytes=24 * 1024 * 1024
        ),
    )(parts, own)


def per_device(rows, cols, weights, rates):
    chunk = weights.shape[1] // rows
    row_index = lax.axis_index("row")
    exchange = [(r * cols + c, c * rows + r) for r in range(rows) for c in range(cols)]
    own = lax.dynamic_slice_in_dim(rates, row_index * chunk, chunk, 1).astype(jnp.float32)

    def local_grad(adjoint, step):
        return (adjoint * (1.0 - own[step] * own[step])).astype(jnp.bfloat16)

    def spread(piece):
        moved = lax.ppermute(piece, ("row", "col"), exchange)
        return lax.all_gather(moved, "col", axis=0, tiled=True)

    grad = spread(local_grad(own[STEPS] - own[0], STEPS))
    grads = [grad]
    for step in range(STEPS, 1, -1):
        partial_sum = lax.dot_general(
            weights, grad, (((0,), (0,)), ((), ())), preferred_element_type=jnp.float32
        ).astype(jnp.bfloat16)
        split = partial_sum.reshape(rows, chunk, -1)
        own_rates = lax.dynamic_slice_in_dim(rates[step - 1], row_index * chunk, chunk, 0)
        grad = spread(exchange_sum(rows, split, own_rates))
        grads.append(grad)
    stacked = jnp.concatenate(grads, axis=1)
    previous = jnp.concatenate([rates[step - 1] for step in range(STEPS, 0, -1)], axis=1)
    return lax.dot_general(
        stacked, previous, (((1,), (1,)), ((), ())), preferred_element_type=jnp.float32
    ).astype(jnp.bfloat16)


def solution(mesh):
    rows, cols = mesh.shape["row"], mesh.shape["col"]

    def body(weights, rates):
        return per_device(rows, cols, weights, rates)

    return jax.shard_map(
        body, mesh=mesh, in_specs=(P("row", "col"), P(None, "col", None)),
        out_specs=P("row", "col"), check_vma=False
    )
```
